32 devices in a mesh: section: 8 (over z, x), dp: 4 (over y, core).
Axes of the slice: x: 2, y: 2, z: 4, core: 2. Of those that a mesh axis runs over, the one named last changes fastest.
Arguments:
- streams: bfloat16 [2, 8, 4, 128, 1024], P(None, 'section', 'dp'), may hold values from -45 to 45
- cotangents: bfloat16 [2, 8, 4, 128, 1024], P(None, 'section', 'dp'), may hold values from -6 to 6
- weights: bfloat16 [8, 1024, 4096], P('section'), may hold values from -0.1875 to 0.1875
- norm_gains: float32 [8, 1024], P('section'), may hold values from 0.25 to 1.75
- segment_ids: int32 [8, 4, 128], P(None, 'dp'), may hold values from 0 to 1, never falling along the last dimension, each value on 1 to 96 neighbouring positions
Outputs:
- out_streams: bfloat16 [2, 8, 4, 128, 1024], P(None, 'section', 'dp')
- out_cotangents: bfloat16 [2, 8, 4, 128, 1024], P(None, 'section', 'dp')
- weight_grads: bfloat16 [8, 1024, 4096], P('section', 'dp')
- gain_grads: float32 [8, 1024], P('section', 'dp')
The draws below stay inside these ranges and needn't reach their ends.
Inputs may be any that keep to these rules, and one draw needn't show every extreme that they name: `segment_ids`: along each row of 128 tokens the document numbers never fall; each row is a 128-token window of packed documents, attention stays inside the window, and each document has 1 to 96 tokens in it.
All inputs are finite; a program needn't handle non-finite values.
Results may differ from the reference program's by a relative error of at most 0.018.
Values may be sent and summed in bfloat16 or wider, within the bound.
A program may use at most 128 MiB of HBM per device.

```python
import math
import jax
import jax.numpy as jnp
import numpy as np
from jax import lax

D = 1024
HEADS = 16
FF = 2048
ROWS = 128
TICKS = 3
SEG_COUNT = 2
SEG_MOST = 96
SECTIONS = 8
REPLICAS = 4
TOKENS_SUMMED = 1536


def draw_streams(key, part):
    subkeys = jax.random.split(key, 3)
    full_shape = (2, SECTIONS, REPLICAS, ROWS, D)
    log_low = math.log(0.3)
    log_high = math.log(3.0)
    row_scale = jnp.exp(jax.random.uniform(subkeys[0], (2, SECTIONS, REPLICAS, ROWS, 1), jnp.float32, log_low, log_high))
    col_scale = jnp.exp(jax.random.uniform(subkeys[1], (2, SECTIONS, REPLICAS, 1, D), jnp.float32, log_low, log_high))
    base_values = jax.random.normal(subkeys[2], full_shape, jnp.float32)
    base_values = jnp.clip(base_values, -5.0, 5.0)
    return (base_values * row_scale * col_scale).astype(jnp.bfloat16)


def block_levels(rng, extent, cuts, least, high):
    def one(dim, shards_of):
        steps = jax.random.uniform(jax.random.fold_in(jax.random.fold_in(rng, 6), dim), (shards_of,), jnp.float32, least / len(cuts), high / len(cuts))
        return jnp.repeat(jnp.exp(steps), extent[dim] // shards_of).reshape((-1,) + (1,) * (len(extent) - dim - 1))

    level = one(*cuts[0])
    for cut in cuts[1:]:
        level = level * one(*cut)
    return level


def profile(number_of, total, most, slope):
    portions = [(1 << 20) // math.isqrt(rank ** slope) + 1 for rank in range(2, number_of + 1)]
    surplus, counts = total - most - (number_of - 1), [1] * (number_of - 1)
    while surplus > 0:
        movable = [i for i in range(number_of - 1) if counts[i] < most]
        mass, remaining = sum([portions[i] for i in movable]), surplus
        for i in movable:
            extra = min(most - counts[i], max(1, remaining * portions[i] // mass), surplus)
            counts[i] = counts[i] + extra
            surplus = surplus - extra
    return np.array([most] + counts)


def ragged(key, amount, total, limit, lean):
    if amount == 2:
        one = jax.random.randint(key, (), max(1, total - limit), min(limit, total - 1) + 1)
        return jnp.stack([one, total - one])
    sizes = jnp.asarray(profile(amount, total, limit, lean), jnp.int32)
    couples = (amount - 1) // 2
    giver, taker = sizes[1:1 + 2 * couples:2], sizes[2:2 + 2 * couples:2]
    room = jnp.minimum(giver - 1, limit - taker)
    passed = jax.random.randint(jax.random.fold_in(key, 1), (couples,), 0, 1 << 20) % (room + 1)
    sizes = sizes.at[1:1 + 2 * couples:2].set(giver - passed).at[2:2 + 2 * couples:2].set(taker + passed)
    return sizes[jax.random.permutation(jax.random.fold_in(key, 2), amount)]


def noise(stream_key, extent, scale, reach, cuts=(), held_as=jnp.bfloat16):
    loudness = block_levels(stream_key, extent, cuts, -0.22, 0.18) if cuts else 1.0
    entries = jax.random.normal(stream_key, extent, jnp.float32) * scale * loudness
    return jnp.minimum(jnp.maximum(entries, -reach), reach).astype(held_as)


def setup_inputs(seed: int = 0) -> dict:
    keys = jax.random.split(jax.random.key(seed), 6)
    return {
        "streams": draw_streams(jax.random.fold_in(keys[5], 71), 0),
        "cotangents": noise(keys[1], (2, SECTIONS, REPLICAS, ROWS, D), 1.0, 6.0, ((1, 8), (2, 4))),
        "weights": noise(keys[2], (SECTIONS, D, 4 * D), D ** -0.5, 0.1875, ((0, 8),)),
        "norm_gains": jnp.clip(1.0 + 0.15 * jax.random.normal(keys[3], (SECTIONS, D), jnp.float32), 0.25, 1.75),
        "segment_ids": jax.vmap(lambda own: jnp.searchsorted(jnp.cumsum(ragged(own, SEG_COUNT, ROWS, SEG_MOST, 2)), jnp.arange(ROWS), side="right"))(jax.random.split(keys[4], SECTIONS * REPLICAS)).reshape((SECTIONS, REPLICAS, ROWS)).astype(jnp.int32),
    }


epsilon = 1e-05
contract_rows = (((0,), (0,)), ((), ()))
contract_cols = (((1,), (1,)), ((), ()))

def rounded(values):
    return lax.optimization_barrier(values.astype(jnp.bfloat16)).astype(jnp.float32)

def normalize(stream, gain_row):
    mean_square = lax.optimization_barrier(jnp.mean(stream * stream, axis=-1, keepdims=True))
    return stream * lax.rsqrt(mean_square + epsilon) * gain_row

def head_norm(values):
    mean_square = lax.optimization_barrier(jnp.mean(values * values, axis=-1, keepdims=True))
    return values * lax.rsqrt(mean_square + epsilon)

def attend(projected, segment_row):
    row_count = projected.shape[0]
    head_size = D // HEADS
    split_heads = projected.reshape(row_count, 3, HEADS, head_size)
    queries = rounded(head_norm(split_heads[:, 0]))
    key_part = rounded(head_norm(split_heads[:, 1]))
    value_part = rounded(split_heads[:, 2])
    scores = jnp.einsum('qhd,khd->hqk', queries, key_part) / math.sqrt(head_size)
    positions = jnp.arange(row_count)
    allowed = (segment_row[:, None] == segment_row[None, :]) & (positions[None, :] <= positions[:, None])
    raised = jnp.where(allowed[None], jnp.exp(scores), 0.0)
    soft_weights = rounded(raised / lax.optimization_barrier(jnp.sum(raised, axis=-1, keepdims=True)))
    mixture = jnp.einsum('hqk,khd->qhd', soft_weights, value_part)
    return mixture.reshape(row_count, D)

def times_transposed(first, second):
    return lax.dot_general(first, second, contract_cols, preferred_element_type=jnp.float32)

def attention_block(state_now, gain_row, weight, segment_row):
    upper_stream, lower_stream, cot_upper, cot_lower = state_now
    stream = upper_stream.astype(jnp.float32)
    normed = normalize(stream, gain_row).astype(jnp.bfloat16)
    projected = jnp.dot(normed, weight[:, :3 * D], preferred_element_type=jnp.float32)
    mixture, core_back = jax.vjp(lambda inner: attend(inner, segment_row), projected)
    mixture = mixture.astype(jnp.bfloat16)
    branch = jnp.dot(mixture, weight[:, 3 * D:], preferred_element_type=jnp.float32)
    restored = (lower_stream.astype(jnp.float32) - branch).astype(jnp.bfloat16)
    grad_mixture = times_transposed(cot_lower, weight[:, 3 * D:])
    grad_projected = core_back(grad_mixture)[0].astype(jnp.bfloat16)
    grad_normed = times_transposed(grad_projected, weight[:, :3 * D])
    grad_stream, grad_gain = jax.vjp(normalize, stream, gain_row)[1](grad_normed)
    cot_new = (cot_upper.astype(jnp.float32) + grad_stream).astype(jnp.bfloat16)
    new_state = (restored, upper_stream, cot_lower, cot_new)
    left_rows = jnp.concatenate([normed, mixture], axis=1)
    right_rows = jnp.concatenate([grad_projected, cot_lower], axis=1)
    return (new_state, left_rows, right_rows, grad_gain)

def mlp_block(state_now, gain_row, weight, segment_row):
    upper_stream, lower_stream, cot_upper, cot_lower = state_now
    stream = upper_stream.astype(jnp.float32)
    normed = normalize(stream, gain_row).astype(jnp.bfloat16)
    before_act = jnp.dot(normed, weight[:, :FF], preferred_element_type=jnp.float32)
    hidden, gelu_back = jax.vjp(jax.nn.gelu, before_act)
    hidden = hidden.astype(jnp.bfloat16)
    branch = times_transposed(hidden, weight[:, FF:])
    restored = (lower_stream.astype(jnp.float32) - branch).astype(jnp.bfloat16)
    grad_hidden = jnp.dot(cot_lower, weight[:, FF:], preferred_element_type=jnp.float32)
    grad_before = gelu_back(grad_hidden)[0].astype(jnp.bfloat16)
    grad_normed = times_transposed(grad_before, weight[:, :FF])
    grad_stream, grad_gain = jax.vjp(normalize, stream, gain_row)[1](grad_normed)
    cot_new = (cot_upper.astype(jnp.float32) + grad_stream).astype(jnp.bfloat16)
    new_state = (restored, upper_stream, cot_lower, cot_new)
    left_rows = jnp.concatenate([normed, cot_lower], axis=1)
    right_rows = jnp.concatenate([grad_before, hidden], axis=1)
    return (new_state, left_rows, right_rows, grad_gain)

def weight_grad(left_first, left_second, right_rows, split):
    first = lax.dot_general(left_first, right_rows[:, :split], contract_rows, preferred_element_type=jnp.float32)
    second = lax.dot_general(left_second, right_rows[:, split:], contract_rows, preferred_element_type=jnp.float32)
    return jnp.concatenate([first, second], axis=1)

def section_pair(items):
    state_pair, weight_pair, gain_pair, segment_pair = items
    outputs = []
    for kind_index, block_fn in enumerate((attention_block, mlp_block)):

        def replica_step(replica_items, block_fn=block_fn, kind_index=kind_index):
            state_now, segment_row = replica_items
            return block_fn(state_now, gain_pair[kind_index], weight_pair[kind_index], segment_row)
        members = tuple((member[kind_index] for member in state_pair))
        outputs.append(lax.map(replica_step, (members, segment_pair[kind_index])))
    return jax.tree.map(lambda first, second: jnp.stack([first, second]), outputs[0], outputs[1])

def reference(streams, cotangents, weights, norm_gains, segment_ids):
    pair_count = SECTIONS // 2

    def paired(array):
        return array.reshape((pair_count, 2) + array.shape[1:])

    def unpaired(array):
        return array.reshape((SECTIONS,) + array.shape[2:])
    state_now = (streams[0], streams[1], cotangents[0], cotangents[1])
    left_ticks, right_ticks = ([], [])
    gain_total = jnp.zeros((SECTIONS, REPLICAS, D), jnp.float32)
    for tick_index in range(TICKS):
        segments_now = jnp.roll(segment_ids, -tick_index, axis=0)
        result = lax.map(section_pair, (tuple((paired(member) for member in state_now)), paired(weights), paired(norm_gains), paired(segments_now)))
        new_state, left_rows, right_rows, grad_gain = jax.tree.map(unpaired, result)
        left_ticks.append(left_rows)
        right_ticks.append(right_rows)
        gain_total = gain_total + grad_gain
        state_now = tuple((jnp.roll(member, -1, axis=0) for member in new_state))
    left_all = jnp.concatenate(left_ticks, axis=2)
    right_all = jnp.concatenate(right_ticks, axis=2)
    grad_scale = 1.0 / math.sqrt(TOKENS_SUMMED)

    def section_grads(items):
        left_pair, right_pair = items
        grads = []
        for kind_index, split in enumerate((3 * D, FF)):

            def replica_grad(replica_items, split=split):
                left_rows, right_rows = replica_items
                return rounded(weight_grad(left_rows[:, :D], left_rows[:, D:], right_rows, split))
            summed = lax.optimization_barrier(jnp.sum(lax.map(replica_grad, (left_pair[kind_index], right_pair[kind_index])), axis=0))
            grads.append((summed * grad_scale).astype(jnp.bfloat16))
        return jnp.stack(grads)
    weight_grads = unpaired(lax.map(section_grads, (paired(left_all), paired(right_all))))
    gain_grads = lax.optimization_barrier(jnp.sum(rounded(gain_total), axis=1)) * grad_scale
    out_streams = jnp.stack([state_now[0], state_now[1]])
    out_cotangents = jnp.stack([state_now[2], state_now[3]])
    return (out_streams, out_cotangents, weight_grads, gain_grads)
```

```python
from functools import partial
import math

import jax
import jax.numpy as jnp
from jax import lax
from jax.experimental import pallas as pl
from jax.experimental.pallas import tpu as pltpu
from jax.sharding import PartitionSpec as P

HEADS = 16
TICKS = 3
CORES = 2

epsilon = 1e-05
GELU_A = math.sqrt(2.0 / math.pi)
GELU_B = 0.044715
MESH = pl.DeviceIdType.MESH
f32 = jnp.float32
bf16 = jnp.bfloat16


def dot_nn(first, second):
    return lax.dot_general(first, second, (((1,), (0,)), ((), ())), preferred_element_type=f32)


def dot_nt(first, second):
    return lax.dot_general(first, second, (((1,), (1,)), ((), ())), preferred_element_type=f32)


def dot_tn(first, second):
    return lax.dot_general(first, second, (((0,), (0,)), ((), ())), preferred_element_type=f32)


def kernel(
    sections, replicas,
    streams, cotangents, weights, gain_ref, segs,
    out_streams, out_cotangents, grads, gain_grads,
    w, y1, y2, c1, c2, proj, dmix,
    right, normed, second, right_all, normed_all, second_all,
    dgain, dgain_send, dgain_all, acc, done,
    w_sem, in_sem, send_sem, recv_sem, own_sem, dp_send, dp_recv, dg_send, dg_recv, fin_send, fin_recv,
):
    s = lax.axis_index("section")
    r = lax.axis_index("dp")
    core = lax.rem(r, CORES)
    chip = r // CORES
    chips = replicas // CORES
    rows, dim = y1.shape[1:]
    part = dim // chips
    wide = right.shape[-1]
    own = dim // replicas
    head = dim // HEADS
    is_att = lax.rem(s, 2) == 0
    before = lax.rem(s + sections - 1, sections)
    before2 = lax.rem(s + sections - 2, sections)
    peers = [lax.rem(r + j, replicas) for j in range(1, replicas)]

    loads = [
        pltpu.make_async_copy(streams.at[0], y1.at[0], in_sem.at[0]),
        pltpu.make_async_copy(cotangents.at[1], c2.at[0], in_sem.at[1]),
        pltpu.make_async_copy(streams.at[1], y2.at[0], in_sem.at[2]),
        pltpu.make_async_copy(cotangents.at[0], c1.at[0], in_sem.at[3]),
    ]
    for copy in loads:
        copy.start()
    w_loads = [
        pltpu.make_async_copy(weights.at[:, pl.ds(j * dim, dim)], w.at[j], w_sem.at[j])
        for j in range(4)
    ]
    for copy in w_loads:
        copy.start()

    barrier = pltpu.get_barrier_semaphore()
    for step in (1, 2, sections - 1, sections - 2):
        pl.semaphore_signal(
            barrier, inc=1, device_id=(lax.rem(s + step, sections), r), device_id_type=MESH
        )
    for peer in peers:
        pl.semaphore_signal(barrier, inc=1, device_id=(s, peer), device_id_type=MESH)
    for copy in loads:
        copy.wait()
    pl.semaphore_wait(barrier, 4 + replicas - 1)

    def hand(src, dst, slot, kind, target):
        return pltpu.make_async_remote_copy(
            src_ref=src, dst_ref=dst.at[slot],
            send_sem=send_sem.at[kind, slot], recv_sem=recv_sem.at[kind, slot],
            device_id=(target, r), device_id_type=MESH,
        )

    hand(y1.at[0], y2, 1, 1, before).start()
    hand(c2.at[0], c1, 1, 2, before).start()
    for copy in w_loads:
        copy.wait()
    dgain[...] = jnp.zeros_like(dgain)

    def rows_of(tick, replica):
        return pl.ds(pl.multiple_of((tick * replicas + replica) * rows, rows), rows)

    def share(tick, j, kind):
        peer = peers[j]
        peer_core = lax.rem(peer, CORES)
        peer_chip = peer // CORES
        if kind == 0:
            src, dst = normed.at[tick, peer_chip], normed_all
        elif kind == 1:
            src, dst = second.at[tick, peer_chip], second_all
        else:
            src, dst = right.at[tick, peer_core], right_all
        return pltpu.make_async_remote_copy(
            src_ref=src, dst_ref=dst.at[rows_of(tick, r)],
            send_sem=dp_send.at[kind, tick, j], recv_sem=dp_recv.at[kind, tick, j],
            device_id=(s, peer), device_id_type=MESH,
        )

    def own_copy(tick, kind):
        if kind == 0:
            src, dst = normed.at[tick, chip], normed_all
        elif kind == 1:
            src, dst = second.at[tick, chip], second_all
        else:
            src, dst = right.at[tick, core], right_all
        return pltpu.make_async_copy(src, dst.at[rows_of(tick, r)], own_sem.at[kind, tick])

    def share_start(tick, kind):
        for j in reversed(range(replicas - 1)):
            share(tick, j, kind).start()
        own_copy(tick, kind).start()

    def tick_body(t, carry):
        @pl.when(t > 0)
        def _():
            hand(y1.at[0], y1, t, 0, before).wait_recv()

        stream = y1[t].astype(f32)
        scale = lax.rsqrt(jnp.mean(stream * stream, axis=-1, keepdims=True) + epsilon)
        n = (stream * scale * gain_ref[...]).astype(bf16)
        for c in range(chips):
            normed[t, c] = n[:, c * part : (c + 1) * part]
        share_start(t, 0)

        @pl.when(t > 0)
        def _():
            hand(c2.at[0], c2, t, 3, before).wait_recv()
            hand(y2.at[0], y2, t, 1, before).wait_recv()
            hand(c1.at[0], c1, t, 2, before).wait_recv()

        @pl.when(is_att)
        def _():
            for j in range(3):
                proj[:, j * dim : (j + 1) * dim] = dot_nn(n, w[j])
            dmix[...] = dot_nt(c2[t], w[3])
            right[t, 1, :, dim:] = c2[t]
            seg = segs[lax.rem(s + t, sections)].astype(f32)
            across = jnp.broadcast_to(seg, (rows, rows))
            row_id = lax.broadcasted_iota(jnp.int32, (rows, rows), 0)
            col_id = lax.broadcasted_iota(jnp.int32, (rows, rows), 1)
            one = ((across == across.T) & (col_id <= row_id)).astype(f32)
            keep = jnp.concatenate([one, one], axis=0)
            lane = lax.broadcasted_iota(jnp.int32, (rows, 2 * head), 1)
            low = lane < head

            def stacked(values):
                return jnp.concatenate(
                    [jnp.where(low, values, 0.0), jnp.where(low, 0.0, values)], axis=0
                )

            def merged(values):
                return jnp.where(low, values[:rows], values[rows:])

            def means(values):
                first = jnp.sum(jnp.where(low, values, 0.0), axis=-1, keepdims=True)
                last = jnp.sum(jnp.where(low, 0.0, values), axis=-1, keepdims=True)
                return first * (1.0 / head), last * (1.0 / head)

            def inv_rms(values):
                first, last = means(values * values)
                return jnp.where(low, lax.rsqrt(first + epsilon), lax.rsqrt(last + epsilon))

            def norm_back(grad, unit, inv):
                first, last = means(grad * unit)
                return inv * (grad - unit * jnp.where(low, first, last))

            def pair(i, carry):
                base = i * 2 * head
                at = [pl.ds(pl.multiple_of(base + j * dim, 2 * head), 2 * head) for j in range(3)]
                q, k = proj[:, at[0]], proj[:, at[1]]
                v = proj[:, at[2]].astype(bf16)
                q_inv, k_inv = inv_rms(q), inv_rms(k)
                q_unit, k_unit = q * q_inv, k * k_inv
                q_two = stacked(q_unit).astype(bf16)
                k_one = k_unit.astype(bf16)
                e = jnp.exp(dot_nt(q_two, k_one) * (1.0 / math.sqrt(head))) * keep
                soft = e * (1.0 / jnp.sum(e, axis=-1, keepdims=True))
                p = soft.astype(bf16)
                o = merged(dot_nn(p, v)).astype(bf16)
                per = part // (2 * head)
                second[t, i // per, :, pl.ds(pl.multiple_of(lax.rem(i, per) * 2 * head, 2 * head), 2 * head)] = o
                do = stacked(dmix[:, at[0]]).astype(bf16)
                dv = dot_tn(p, do)
                dp = dot_nt(do, v).astype(bf16).astype(f32)
                ds = soft * (dp - jnp.sum(dp * soft, axis=-1, keepdims=True))
                ds = (ds * (1.0 / math.sqrt(head))).astype(bf16)
                dq = merged(dot_nn(ds, k_one)).astype(bf16).astype(f32)
                dk = dot_tn(ds, q_two).astype(bf16).astype(f32)
                right[t, 0, :, at[0]] = norm_back(dq, q_unit, q_inv).astype(bf16)
                right[t, 0, :, at[1]] = norm_back(dk, k_unit, k_inv).astype(bf16)
                right[t, 1, :, at[0]] = dv.astype(bf16)
                return carry

            lax.fori_loop(0, HEADS // 2, pair, 0, unroll=2)

        @pl.when(jnp.logical_not(is_att))
        def _():
            for c in range(chips):
                second[t, c] = c2[t, :, c * part : (c + 1) * part]
            for j in range(2):
                at = pl.ds(j * dim, dim)
                proj[:, at] = dot_nn(n, w[j])
                dmix[...] = dot_nn(c2[t], w[2 + j])

                def strip(i, carry):
                    cols = pl.ds(pl.multiple_of(i * 256, 256), 256)
                    to = pl.ds(pl.multiple_of(j * dim + i * 256, 256), 256)
                    x = proj[:, to]
                    square = x * x
                    tanh = jnp.tanh(GELU_A * x * (1.0 + GELU_B * square))
                    half = 0.5 * (1.0 + tanh)
                    slope = half + 0.5 * x * (1.0 - tanh * tanh) * GELU_A * (1.0 + 3.0 * GELU_B * square)
                    right[t, 1, :, to] = (x * half).astype(bf16)
                    right[t, 0, :, to] = (slope * dmix[:, cols]).astype(bf16)
                    return carry

                lax.fori_loop(0, dim // 256, strip, 0)

        share_start(t, 2)
        share_start(t, 1)

        @pl.when(is_att)
        def _():
            branch = dot_nn(second[t, 0], w[3, :part])
            for c in range(1, chips):
                branch = branch + dot_nn(second[t, c], w[3, c * part : (c + 1) * part])
            y1[t + 1 + TICKS] = (y2[t].astype(f32) - branch).astype(bf16)

        @pl.when(jnp.logical_not(is_att))
        def _():
            branch = dot_nt(right[t, 1, :, :dim], w[2]) + dot_nt(right[t, 1, :, dim:], w[3])
            y1[t + 1 + TICKS] = (y2[t].astype(f32) - branch).astype(bf16)

        made, cot = t + 1 + TICKS, t + 1 + TICKS
        hand(y1.at[made], y1, t + 1, 0, before).start()

        @pl.when(is_att)
        def _():
            dmix[...] = (
                dot_nt(right[t, 0, :, :dim], w[0])
                + dot_nt(right[t, 0, :, dim:], w[1])
                + dot_nt(right[t, 1, :, :dim], w[2])
            )

        @pl.when(jnp.logical_not(is_att))
        def _():
            dmix[...] = dot_nt(right[t, 0, :, :dim], w[0]) + dot_nt(right[t, 0, :, dim:], w[1])

        dn = dmix[...]
        unit = y1[t].astype(f32) * scale
        dgain[...] += jnp.sum(dn * unit, axis=0, keepdims=True)
        weighted = dn * gain_ref[...]
        du = scale * (weighted - unit * jnp.mean(weighted * unit, axis=-1, keepdims=True))
        c2[cot] = (c1[t].astype(f32) + du).astype(bf16)
        hand(c2.at[cot], c2, t + 1, 3, before).start()

        @pl.when(t < TICKS - 1)
        def _():
            hand(y1.at[made], y2, t + 2, 1, before2).start()
            hand(c2.at[cot], c1, t + 2, 2, before2).start()

        return carry

    lax.fori_loop(0, TICKS, tick_body, 0)

    total = dgain[...].astype(bf16).astype(f32)
    for q in range(replicas):
        dgain_send[q] = jnp.broadcast_to(total[:, q * own : (q + 1) * own], dgain_send.shape[1:])

    def gain_copy(j):
        return pltpu.make_async_remote_copy(
            src_ref=dgain_send.at[peers[j]], dst_ref=dgain_all.at[r],
            send_sem=dg_send.at[j], recv_sem=dg_recv.at[j],
            device_id=(s, peers[j]), device_id_type=MESH,
        )

    for j in range(replicas - 1):
        gain_copy(j).start()
    dgain_all[r] = dgain_send[r]

    def share_wait(tick):
        for kind in (0, 2, 1):
            own_copy(tick, kind).wait()
            for j in reversed(range(replicas - 1)):
                share(tick, j, kind).wait()

    tokens = replicas * rows
    chunk = 256

    def accumulate(first, count, fresh):
        span = pl.ds(first * tokens, count * tokens)

        def strip(i, carry):
            cols = pl.ds(pl.multiple_of(i * chunk, chunk), chunk)
            use_normed = jnp.logical_or(core == 0, jnp.logical_and(is_att, i < dim // chunk))

            @pl.when(use_normed)
            def _():
                value = dot_tn(normed_all[span], right_all[span, cols])
                acc[:, cols] = value if fresh else acc[:, cols] + value

            @pl.when(jnp.logical_not(use_normed))
            def _():
                value = dot_tn(second_all[span], right_all[span, cols])
                acc[:, cols] = value if fresh else acc[:, cols] + value

            return carry

        lax.fori_loop(0, wide // chunk, strip, 0)

    for tick in range(TICKS - 1):
        share_wait(tick)
    accumulate(0, TICKS - 1, True)
    share_wait(TICKS - 1)
    accumulate(TICKS - 1, 1, False)

    grad_scale = 1.0 / math.sqrt(TICKS * rows * replicas)
    mine = pl.ds(pl.multiple_of(core * own, own), own)
    cols = pl.ds(pl.multiple_of(core * wide, wide), wide)
    other = CORES - 1 - core
    done[...] = (acc[pl.ds(pl.multiple_of(other * own, own), own), :] * grad_scale).astype(bf16)
    final = pltpu.make_async_remote_copy(
        src_ref=done, dst_ref=grads.at[:, cols],
        send_sem=fin_send, recv_sem=fin_recv,
        device_id=(s, chip * CORES + other), device_id_type=MESH,
    )
    final.start()
    grads[:, cols] = (acc[mine, :] * grad_scale).astype(bf16)

    for j in range(replicas - 1):
        gain_copy(j).wait()
    gain_sum = dgain_all[0, :1]
    for q in range(1, replicas):
        gain_sum = gain_sum + dgain_all[q, :1]
    gain_grads[...] = gain_sum * grad_scale

    hand(y1.at[0], y1, TICKS, 0, before).wait_recv()
    hand(c2.at[0], c2, TICKS, 3, before).wait_recv()
    hand(y2.at[0], y2, TICKS, 1, before).wait_recv()
    hand(c1.at[0], c1, TICKS, 2, before).wait_recv()
    out_streams[0] = y1[TICKS]
    out_streams[1] = y2[TICKS]
    out_cotangents[0] = c1[TICKS]
    out_cotangents[1] = c2[TICKS]
    for slot in range(1, TICKS + 1):
        hand(y1.at[0], y1, slot, 0, before).wait_send()
        hand(c2.at[0], c2, slot, 3, before).wait_send()
        hand(y1.at[0], y2, slot, 1, before).wait_send()
        hand(c2.at[0], c1, slot, 2, before).wait_send()
    final.wait()


def shards(streams, cotangents, weights, norm_gains, segment_ids):
    sections = lax.axis_size("section")
    replicas = lax.axis_size("dp")
    chips = replicas // CORES
    rows, dim = streams.shape[3:]
    full = weights.shape[2]
    wide = full // CORES
    part = dim // chips
    own = dim // replicas
    tokens = TICKS * replicas * rows
    dma = pltpu.SemaphoreType.DMA
    vmem = pl.BlockSpec(memory_space=pltpu.VMEM)
    hbm = pl.BlockSpec(memory_space=pl.ANY)
    flops = 2 * TICKS * rows * dim * full * 3
    out_streams, out_cotangents, grads, gains = pl.pallas_call(
        partial(kernel, sections, replicas),
        out_shape=(
            jax.ShapeDtypeStruct((2, rows, dim), bf16),
            jax.ShapeDtypeStruct((2, rows, dim), bf16),
            jax.ShapeDtypeStruct((own, full), bf16),
            jax.ShapeDtypeStruct((1, own), f32),
        ),
        in_specs=[hbm, hbm, hbm, vmem, vmem],
        out_specs=(vmem, vmem, vmem, vmem),
        scratch_shapes=[
            pltpu.VMEM((4, dim, dim), bf16),
            pltpu.VMEM((2 * TICKS + 1, rows, dim), bf16),
            pltpu.VMEM((TICKS + 1, rows, dim), bf16),
            pltpu.VMEM((TICKS + 1, rows, dim), bf16),
            pltpu.VMEM((2 * TICKS + 1, rows, dim), bf16),
            pltpu.VMEM((rows, 3 * dim), f32),
            pltpu.VMEM((rows, dim), f32),
            pltpu.VMEM((TICKS, CORES, rows, wide), bf16),
            pltpu.VMEM((TICKS, chips, rows, part), bf16),
            pltpu.VMEM((TICKS, chips, rows, part), bf16),
            pltpu.VMEM((tokens, wide), bf16),
            pltpu.VMEM((tokens, part), bf16),
            pltpu.VMEM((tokens, part), bf16),
            pltpu.VMEM((1, dim), f32),
            pltpu.VMEM((replicas, 8, own), f32),
            pltpu.VMEM((replicas, 8, own), f32),
            pltpu.VMEM((part, wide), f32),
            pltpu.VMEM((own, wide), bf16),
            dma((4,)),
            dma((4,)),
            dma((4, TICKS + 1)),
            dma((4, TICKS + 1)),
            dma((3, TICKS)),
            dma((3, TICKS, replicas - 1)),
            dma((3, TICKS, replicas - 1)),
            dma((replicas - 1,)),
            dma((replicas - 1,)),
            dma,
            dma,
        ],
        compiler_params=pltpu.CompilerParams(
            collective_id=0, has_side_effects=True, vmem_limit_bytes=56 * 1024 * 1024
        ),
        cost_estimate=pl.CostEstimate(
            flops=flops, bytes_accessed=2 * dim * full, transcendentals=0
        ),
        name="ticks",
    )(
        streams[:, 0, 0],
        cotangents[:, 0, 0],
        weights[0],
        norm_gains,
        segment_ids,
    )
    return (
        out_streams[:, None, None],
        out_cotangents[:, None, None],
        grads[None],
        gains,
    )


def solution(mesh):
    placed = (
        P(None, "section", "dp", None, None),
        P(None, "section", "dp", None, None),
        P("section", None, None),
        P("section", None),
        P(None, "dp", None),
    )
    return jax.shard_map(
        shards,
        mesh=mesh,
        in_specs=placed,
        out_specs=(
            P(None, "section", "dp", None, None),
            P(None, "section", "dp", None, None),
            P("section", "dp", None),
            P("section", "dp"),
        ),
        check_vma=False,
    )
```

```python
from functools import partial
import math

import jax
import jax.numpy as jnp
from jax import lax
from jax.experimental import pallas as pl
from jax.experimental.pallas import tpu as pltpu
from jax.sharding import PartitionSpec as P

HEADS = 16
TICKS = 3
CORES = 2

epsilon = 1e-05
GELU_A = math.sqrt(2.0 / math.pi)
GELU_B = 0.044715
MESH = pl.DeviceIdType.MESH
f32 = jnp.float32
bf16 = jnp.bfloat16


def dot_nn(first, second):
    return lax.dot_general(first, second, (((1,), (0,)), ((), ())), preferred_element_type=f32)


def dot_nt(first, second):
    return lax.dot_general(first, second, (((1,), (1,)), ((), ())), preferred_element_type=f32)


def dot_tn(first, second):
    return lax.dot_general(first, second, (((0,), (0,)), ((), ())), preferred_element_type=f32)


def kernel(
    sections, replicas,
    streams, cotangents, weights, gain_ref, segs,
    out_streams, out_cotangents, grads, gain_grads,
    w, y1, y2, c1, c2, proj, dmix,
    right, normed, second, right_all, normed_all, second_all,
    dgain, dgain_send, dgain_all, acc, done,
    w_sem, in_sem, send_sem, recv_sem, own_sem, dp_send, dp_recv, fwd_send, fwd_recv, dg_send, dg_recv, fin_send, fin_recv,
):
    s = lax.axis_index("section")
    r = lax.axis_index("dp")
    core = lax.rem(r, CORES)
    chip = r // CORES
    chips = replicas // CORES
    rows, dim = y1.shape[1:]
    part = dim // chips
    wide = right.shape[-1]
    own = dim // replicas
    head = dim // HEADS
    is_att = lax.rem(s, 2) == 0
    before = lax.rem(s + sections - 1, sections)
    before2 = lax.rem(s + sections - 2, sections)
    peers = [lax.rem(r + j, replicas) for j in range(1, replicas)]

    loads = [
        pltpu.make_async_copy(streams.at[0], y1.at[0], in_sem.at[0]),
        pltpu.make_async_copy(cotangents.at[1], c2.at[0], in_sem.at[1]),
        pltpu.make_async_copy(streams.at[1], y2.at[0], in_sem.at[2]),
        pltpu.make_async_copy(cotangents.at[0], c1.at[0], in_sem.at[3]),
    ]
    for copy in loads:
        copy.start()
    w_loads = [
        pltpu.make_async_copy(weights.at[:, pl.ds(j * dim, dim)], w.at[j], w_sem.at[j])
        for j in range(4)
    ]
    for copy in w_loads:
        copy.start()

    barrier = pltpu.get_barrier_semaphore()
    for step in (1, 2, sections - 1, sections - 2):
        pl.semaphore_signal(
            barrier, inc=1, device_id=(lax.rem(s + step, sections), r), device_id_type=MESH
        )
    for peer in peers:
        pl.semaphore_signal(barrier, inc=1, device_id=(s, peer), device_id_type=MESH)
    for copy in loads:
        copy.wait()
    pl.semaphore_wait(barrier, 4 + replicas - 1)

    def hand(src, dst, slot, kind, target):
        return pltpu.make_async_remote_copy(
            src_ref=src, dst_ref=dst.at[slot],
            send_sem=send_sem.at[kind, slot], recv_sem=recv_sem.at[kind, slot],
            device_id=(target, r), device_id_type=MESH,
        )

    hand(y1.at[0], y2, 1, 1, before).start()
    hand(c2.at[0], c1, 1, 2, before).start()
    for copy in w_loads:
        copy.wait()
    dgain[...] = jnp.zeros_like(dgain)

    def rows_of(tick, replica):
        return pl.ds(pl.multiple_of((tick * replicas + replica) * rows, rows), rows)

    def share(tick, j, kind):
        peer = peers[j]
        peer_core = lax.rem(peer, CORES)
        peer_chip = peer // CORES
        rows_here = rows_of(tick, r)
        if kind == 0:
            src, dst = normed.at[tick, peer_chip], normed_all.at[rows_here]
        elif kind == 1:
            src, dst = second.at[tick, peer_chip], second_all.at[rows_here]
        else:
            cols = pl.ds((kind - 2) * dim, dim)
            src, dst = right.at[tick, peer_core, :, cols], right_all.at[rows_here, cols]
        return pltpu.make_async_remote_copy(
            src_ref=src, dst_ref=dst,
            send_sem=dp_send.at[kind, tick, j], recv_sem=dp_recv.at[kind, tick, j],
            device_id=(s, peer), device_id_type=MESH,
        )

    partner = chip * CORES + CORES - 1 - core
    offsets = [CORES * q for q in range(1, chips)]

    def forward(tick, q):
        source = lax.rem(r + replicas - offsets[q], replicas)
        span = rows_of(tick, source)
        return pltpu.make_async_remote_copy(
            src_ref=normed_all.at[span], dst_ref=normed_all.at[span],
            send_sem=fwd_send.at[tick, q], recv_sem=fwd_recv.at[tick, q],
            device_id=(s, partner), device_id_type=MESH,
        )

    def own_copy(tick, kind):
        if kind == 0:
            src, dst = normed.at[tick, chip], normed_all
        elif kind == 1:
            src, dst = second.at[tick, chip], second_all
        else:
            src, dst = right.at[tick, core], right_all
        return pltpu.make_async_copy(src, dst.at[rows_of(tick, r)], own_sem.at[kind, tick])

    def wanted(j):
        return lax.rem(peers[j], CORES) == CORES - 1

    def near(j):
        return peers[j] == partner

    def norm_start(tick):
        for j in reversed(range(replicas - 1)):
            if j + 1 in offsets:
                share(tick, j, 0).start()
            else:
                @pl.when(near(j))
                def _(j=j):
                    share(tick, j, 0).start()
        own_copy(tick, 0).start()

    def second_start(tick):
        for j in reversed(range(replicas - 1)):
            @pl.when(wanted(j))
            def _(j=j):
                share(tick, j, 1).start()
        own_copy(tick, 1).start()

    def right_start(tick, kind, last_core):
        for j in reversed(range(replicas - 1)):
            @pl.when(wanted(j) if last_core else jnp.logical_not(wanted(j)))
            def _(j=j):
                share(tick, j, kind).start()

    def tick_body(t, carry):
        @pl.when(t > 0)
        def _():
            hand(y1.at[0], y1, t, 0, before).wait_recv()

        stream = y1[t].astype(f32)
        scale = lax.rsqrt(jnp.mean(stream * stream, axis=-1, keepdims=True) + epsilon)
        n = (stream * scale * gain_ref[...]).astype(bf16)
        for c in range(chips):
            normed[t, c] = n[:, c * part : (c + 1) * part]
        norm_start(t)

        @pl.when(t > 0)
        def _():
            hand(c2.at[0], c2, t, 3, before).wait_recv()
            hand(y2.at[0], y2, t, 1, before).wait_recv()
            hand(c1.at[0], c1, t, 2, before).wait_recv()

        @pl.when(is_att)
        def _():
            right[t, 1, :, dim:] = c2[t]
            right_start(t, 3, True)
            for j in range(3):
                proj[:, j * dim : (j + 1) * dim] = dot_nn(n, w[j])
            dmix[...] = dot_nt(c2[t], w[3])
            seg = segs[lax.rem(s + t, sections)].astype(f32)
            across = jnp.broadcast_to(seg, (rows, rows))
            row_id = lax.broadcasted_iota(jnp.int32, (rows, rows), 0)
            col_id = lax.broadcasted_iota(jnp.int32, (rows, rows), 1)
            one = ((across == across.T) & (col_id <= row_id)).astype(f32)
            keep = jnp.concatenate([one, one], axis=0)
            lane = lax.broadcasted_iota(jnp.int32, (rows, 2 * head), 1)
            low = lane < head

            def stacked(values):
                return jnp.concatenate(
                    [jnp.where(low, values, 0.0), jnp.where(low, 0.0, values)], axis=0
                )

            def merged(values):
                return jnp.where(low, values[:rows], values[rows:])

            def means(values):
                first = jnp.sum(jnp.where(low, values, 0.0), axis=-1, keepdims=True)
                last = jnp.sum(jnp.where(low, 0.0, values), axis=-1, keepdims=True)
                return first * (1.0 / head), last * (1.0 / head)

            def inv_rms(values):
                first, last = means(values * values)
                return jnp.where(low, lax.rsqrt(first + epsilon), lax.rsqrt(last + epsilon))

            def norm_back(grad, unit, inv):
                first, last = means(grad * unit)
                return inv * (grad - unit * jnp.where(low, first, last))

            def pair(i, carry):
                base = i * 2 * head
                at = [pl.ds(pl.multiple_of(base + j * dim, 2 * head), 2 * head) for j in range(3)]
                q, k = proj[:, at[0]], proj[:, at[1]]
                v = proj[:, at[2]].astype(bf16)
                q_inv, k_inv = inv_rms(q), inv_rms(k)
                q_unit, k_unit = q * q_inv, k * k_inv
                q_two = stacked(q_unit).astype(bf16)
                k_one = k_unit.astype(bf16)
                e = jnp.exp(dot_nt(q_two, k_one) * (1.0 / math.sqrt(head))) * keep
                soft = e * (1.0 / jnp.sum(e, axis=-1, keepdims=True))
                p = soft.astype(bf16)
                o = merged(dot_nn(p, v)).astype(bf16)
                per = part // (2 * head)
                second[t, i // per, :, pl.ds(pl.multiple_of(lax.rem(i, per) * 2 * head, 2 * head), 2 * head)] = o
                do = stacked(dmix[:, at[0]]).astype(bf16)
                dv = dot_tn(p, do)
                dp = dot_nt(do, v).astype(bf16).astype(f32)
                ds = soft * (dp - jnp.sum(dp * soft, axis=-1, keepdims=True))
                ds = (ds * (1.0 / math.sqrt(head))).astype(bf16)
                dq = merged(dot_nn(ds, k_one)).astype(bf16).astype(f32)
                dk = dot_tn(ds, q_two).astype(bf16).astype(f32)
                right[t, 0, :, at[0]] = norm_back(dq, q_unit, q_inv).astype(bf16)
                right[t, 0, :, at[1]] = norm_back(dk, k_unit, k_inv).astype(bf16)
                right[t, 1, :, at[0]] = dv.astype(bf16)
                return carry

            lax.fori_loop(0, HEADS // 2, pair, 0, unroll=4)
            right_start(t, 2, False)
            right_start(t, 3, False)
            right_start(t, 2, True)
            second_start(t)

        @pl.when(jnp.logical_not(is_att))
        def _():
            for c in range(chips):
                second[t, c] = c2[t, :, c * part : (c + 1) * part]
            second_start(t)
            for j in range(2):
                at = pl.ds(j * dim, dim)
                proj[:, at] = dot_nn(n, w[j])
                dmix[...] = dot_nn(c2[t], w[2 + j])

                def strip(i, carry):
                    cols = pl.ds(pl.multiple_of(i * 256, 256), 256)
                    to = pl.ds(pl.multiple_of(j * dim + i * 256, 256), 256)
                    x = proj[:, to]
                    square = x * x
                    tanh = jnp.tanh(GELU_A * x * (1.0 + GELU_B * square))
                    half = 0.5 * (1.0 + tanh)
                    slope = half + 0.5 * x * (1.0 - tanh * tanh) * GELU_A * (1.0 + 3.0 * GELU_B * square)
                    right[t, 1, :, to] = (x * half).astype(bf16)
                    right[t, 0, :, to] = (slope * dmix[:, cols]).astype(bf16)
                    return carry

                lax.fori_loop(0, dim // 256, strip, 0)
                right_start(t, 2 + j, False)
                right_start(t, 2 + j, True)

        own_copy(t, 2).start()

        @pl.when(is_att)
        def _():
            branch = dot_nn(second[t, 0], w[3, :part])
            for c in range(1, chips):
                branch = branch + dot_nn(second[t, c], w[3, c * part : (c + 1) * part])
            y1[t + 1 + TICKS] = (y2[t].astype(f32) - branch).astype(bf16)

        @pl.when(jnp.logical_not(is_att))
        def _():
            branch = dot_nt(right[t, 1, :, :dim], w[2]) + dot_nt(right[t, 1, :, dim:], w[3])
            y1[t + 1 + TICKS] = (y2[t].astype(f32) - branch).astype(bf16)

        made, cot = t + 1 + TICKS, t + 1 + TICKS
        hand(y1.at[made], y1, t + 1, 0, before).start()

        @pl.when(is_att)
        def _():
            dmix[...] = (
                dot_nt(right[t, 0, :, :dim], w[0])
                + dot_nt(right[t, 0, :, dim:], w[1])
                + dot_nt(right[t, 1, :, :dim], w[2])
            )

        @pl.when(jnp.logical_not(is_att))
        def _():
            dmix[...] = dot_nt(right[t, 0, :, :dim], w[0]) + dot_nt(right[t, 0, :, dim:], w[1])

        dn = dmix[...]
        unit = y1[t].astype(f32) * scale
        dgain[...] += jnp.sum(dn * unit, axis=0, keepdims=True)
        weighted = dn * gain_ref[...]
        du = scale * (weighted - unit * jnp.mean(weighted * unit, axis=-1, keepdims=True))
        c2[cot] = (c1[t].astype(f32) + du).astype(bf16)
        hand(c2.at[cot], c2, t + 1, 3, before).start()

        @pl.when(t < TICKS - 1)
        def _():
            hand(y1.at[made], y2, t + 2, 1, before2).start()
            hand(c2.at[cot], c1, t + 2, 2, before2).start()

        for q in range(chips - 1):
            share(t, offsets[q] - 1, 0).wait_recv()
            forward(t, q).start()
        return carry

    lax.fori_loop(0, TICKS, tick_body, 0)

    total = dgain[...].astype(bf16).astype(f32)
    for q in range(replicas):
        dgain_send[q] = jnp.broadcast_to(total[:, q * own : (q + 1) * own], dgain_send.shape[1:])

    def gain_copy(j):
        return pltpu.make_async_remote_copy(
            src_ref=dgain_send.at[peers[j]], dst_ref=dgain_all.at[r],
            send_sem=dg_send.at[j], recv_sem=dg_recv.at[j],
            device_id=(s, peers[j]), device_id_type=MESH,
        )

    for j in range(replicas - 1):
        gain_copy(j).start()
    dgain_all[r] = dgain_send[r]

    def share_wait(tick):
        for kind in (0, 2, 1):
            own_copy(tick, kind).wait()
        for q in range(chips - 1):
            share(tick, offsets[q] - 1, 0).wait_send()
            forward(tick, q).wait()
        for j in reversed(range(replicas - 1)):
            if j + 1 not in offsets:
                @pl.when(near(j))
                def _(j=j):
                    share(tick, j, 0).wait_send()

                @pl.when(lax.rem(r + replicas - j - 1, replicas) == partner)
                def _(j=j):
                    share(tick, j, 0).wait_recv()

            @pl.when(wanted(j))
            def _(j=j):
                share(tick, j, 1).wait_send()

            @pl.when(core == CORES - 1)
            def _(j=j):
                share(tick, j, 1).wait_recv()

            share(tick, j, 3).wait()
            share(tick, j, 2).wait()

    tokens = replicas * rows
    chunk = 256

    def accumulate(first, count, fresh):
        span = pl.ds(first * tokens, count * tokens)

        def strip(i, carry):
            cols = pl.ds(pl.multiple_of(i * chunk, chunk), chunk)
            use_normed = jnp.logical_or(core == 0, jnp.logical_and(is_att, i < dim // chunk))

            @pl.when(use_normed)
            def _():
                value = dot_tn(normed_all[span], right_all[span, cols])
                acc[:, cols] = value if fresh else acc[:, cols] + value

            @pl.when(jnp.logical_not(use_normed))
            def _():
                value = dot_tn(second_all[span], right_all[span, cols])
                acc[:, cols] = value if fresh else acc[:, cols] + value

            return carry

        lax.fori_loop(0, wide // chunk, strip, 0)

    for tick in range(TICKS - 1):
        share_wait(tick)
    accumulate(0, TICKS - 1, True)
    share_wait(TICKS - 1)
    accumulate(TICKS - 1, 1, False)

    grad_scale = 1.0 / math.sqrt(TICKS * rows * replicas)
    mine = pl.ds(pl.multiple_of(core * own, own), own)
    cols = pl.ds(pl.multiple_of(core * wide, wide), wide)
    other = CORES - 1 - core
    done[...] = (acc[pl.ds(pl.multiple_of(other * own, own), own), :] * grad_scale).astype(bf16)
    final = pltpu.make_async_remote_copy(
        src_ref=done, dst_ref=grads.at[:, cols],
        send_sem=fin_send, recv_sem=fin_recv,
        device_id=(s, chip * CORES + other), device_id_type=MESH,
    )
    final.start()
    grads[:, cols] = (acc[mine, :] * grad_scale).astype(bf16)

    for j in range(replicas - 1):
        gain_copy(j).wait()
    gain_sum = dgain_all[0, :1]
    for q in range(1, replicas):
        gain_sum = gain_sum + dgain_all[q, :1]
    gain_grads[...] = gain_sum * grad_scale

    hand(y1.at[0], y1, TICKS, 0, before).wait_recv()
    hand(c2.at[0], c2, TICKS, 3, before).wait_recv()
    hand(y2.at[0], y2, TICKS, 1, before).wait_recv()
    hand(c1.at[0], c1, TICKS, 2, before).wait_recv()
    out_streams[0] = y1[TICKS]
    out_streams[1] = y2[TICKS]
    out_cotangents[0] = c1[TICKS]
    out_cotangents[1] = c2[TICKS]
    for slot in range(1, TICKS + 1):
        hand(y1.at[0], y1, slot, 0, before).wait_send()
        hand(c2.at[0], c2, slot, 3, before).wait_send()
        hand(y1.at[0], y2, slot, 1, before).wait_send()
        hand(c2.at[0], c1, slot, 2, before).wait_send()
    final.wait()


def shards(streams, cotangents, weights, norm_gains, segment_ids):
    sections = lax.axis_size("section")
    replicas = lax.axis_size("dp")
    chips = replicas // CORES
    rows, dim = streams.shape[3:]
    full = weights.shape[2]
    wide = full // CORES
    part = dim // chips
    own = dim // replicas
    tokens = TICKS * replicas * rows
    dma = pltpu.SemaphoreType.DMA
    vmem = pl.BlockSpec(memory_space=pltpu.VMEM)
    hbm = pl.BlockSpec(memory_space=pl.ANY)
    flops = 2 * TICKS * rows * dim * full * 3
    out_streams, out_cotangents, grads, gains = pl.pallas_call(
        partial(kernel, sections, replicas),
        out_shape=(
            jax.ShapeDtypeStruct((2, rows, dim), bf16),
            jax.ShapeDtypeStruct((2, rows, dim), bf16),
            jax.ShapeDtypeStruct((own, full), bf16),
            jax.ShapeDtypeStruct((1, own), f32),
        ),
        in_specs=[hbm, hbm, hbm, vmem, vmem],
        out_specs=(vmem, vmem, vmem, vmem),
        scratch_shapes=[
            pltpu.VMEM((4, dim, dim), bf16),
            pltpu.VMEM((2 * TICKS + 1, rows, dim), bf16),
            pltpu.VMEM((TICKS + 1, rows, dim), bf16),
            pltpu.VMEM((TICKS + 1, rows, dim), bf16),
            pltpu.VMEM((2 * TICKS + 1, rows, dim), bf16),
            pltpu.VMEM((rows, 3 * dim), f32),
            pltpu.VMEM((rows, dim), f32),
            pltpu.VMEM((TICKS, CORES, rows, wide), bf16),
            pltpu.VMEM((TICKS, chips, rows, part), bf16),
            pltpu.VMEM((TICKS, chips, rows, part), bf16),
            pltpu.VMEM((tokens, wide), bf16),
            pltpu.VMEM((tokens, part), bf16),
            pltpu.VMEM((tokens, part), bf16),
            pltpu.VMEM((1, dim), f32),
            pltpu.VMEM((replicas, 8, own), f32),
            pltpu.VMEM((replicas, 8, own), f32),
            pltpu.VMEM((part, wide), f32),
            pltpu.VMEM((own, wide), bf16),
            dma((4,)),
            dma((4,)),
            dma((4, TICKS + 1)),
            dma((4, TICKS + 1)),
            dma((3, TICKS)),
            dma((4, TICKS, replicas - 1)),
            dma((4, TICKS, replicas - 1)),
            dma((TICKS, chips - 1)),
            dma((TICKS, chips - 1)),
            dma((replicas - 1,)),
            dma((replicas - 1,)),
            dma,
            dma,
        ],
        compiler_params=pltpu.CompilerParams(
            collective_id=0, has_side_effects=True, vmem_limit_bytes=56 * 1024 * 1024
        ),
        cost_estimate=pl.CostEstimate(
            flops=flops, bytes_accessed=2 * dim * full, transcendentals=0
        ),
        name="ticks",
    )(
        streams[:, 0, 0],
        cotangents[:, 0, 0],
        weights[0],
        norm_gains,
        segment_ids,
    )
    return (
        out_streams[:, None, None],
        out_cotangents[:, None, None],
        grads[None],
        gains,
    )


def solution(mesh):
    placed = (
        P(None, "section", "dp", None, None),
        P(None, "section", "dp", None, None),
        P("section", None, None),
        P("section", None),
        P(None, "dp", None),
    )
    return jax.shard_map(
        shards,
        mesh=mesh,
        in_specs=placed,
        out_specs=(
            P(None, "section", "dp", None, None),
            P(None, "section", "dp", None, None),
            P("section", "dp", None),
            P("section", "dp"),
        ),
        check_vma=False,
    )
```

```python
from functools import partial
import math

import jax
import jax.numpy as jnp
from jax import lax
from jax.experimental import pallas as pl
from jax.experimental.pallas import tpu as pltpu
from jax.sharding import PartitionSpec as P

HEADS = 16
TICKS = 3
CORES = 2

epsilon = 1e-05
GELU_A = math.sqrt(2.0 / math.pi)
GELU_B = 0.044715
MESH = pl.DeviceIdType.MESH
f32 = jnp.float32
bf16 = jnp.bfloat16


def dot_nn(first, second):
    return lax.dot_general(first, second, (((1,), (0,)), ((), ())), preferred_element_type=f32)


def dot_nt(first, second):
    return lax.dot_general(first, second, (((1,), (1,)), ((), ())), preferred_element_type=f32)


def dot_tn(first, second):
    return lax.dot_general(first, second, (((0,), (0,)), ((), ())), preferred_element_type=f32)


def kernel(
    sections, replicas,
    streams, cotangents, weights, gain_ref, segs,
    out_streams, out_cotangents, grads, gain_grads,
    w, y1, y2, c1, c2, proj, dmix,
    right, normed, second, right_all, normed_all, second_all,
    dgain, dgain_send, dgain_all, acc, done,
    w_sem, in_sem, send_sem, recv_sem, own_sem, dp_send, dp_recv, fwd_send, fwd_recv, dg_send, dg_recv, fin_send, fin_recv,
):
    s = lax.axis_index("section")
    r = lax.axis_index("dp")
    core = lax.rem(r, CORES)
    chip = r // CORES
    chips = replicas // CORES
    rows, dim = y1.shape[1:]
    part = dim // chips
    wide = right.shape[-1]
    own = dim // replicas
    head = dim // HEADS
    is_att = lax.rem(s, 2) == 0
    before = lax.rem(s + sections - 1, sections)
    before2 = lax.rem(s + sections - 2, sections)
    peers = [lax.rem(r + j, replicas) for j in range(1, replicas)]

    loads = [
        pltpu.make_async_copy(streams.at[0], y1.at[0], in_sem.at[0]),
        pltpu.make_async_copy(cotangents.at[1], c2.at[0], in_sem.at[1]),
        pltpu.make_async_copy(streams.at[1], y2.at[0], in_sem.at[2]),
        pltpu.make_async_copy(cotangents.at[0], c1.at[0], in_sem.at[3]),
    ]
    for copy in loads:
        copy.start()
    w_loads = [
        pltpu.make_async_copy(weights.at[:, pl.ds(j * dim, dim)], w.at[j], w_sem.at[j])
        for j in range(4)
    ]
    for copy in w_loads:
        copy.start()

    barrier = pltpu.get_barrier_semaphore()
    for step in (1, 2, sections - 1, sections - 2):
        pl.semaphore_signal(
            barrier, inc=1, device_id=(lax.rem(s + step, sections), r), device_id_type=MESH
        )
    for peer in peers:
        pl.semaphore_signal(barrier, inc=1, device_id=(s, peer), device_id_type=MESH)
    for copy in loads:
        copy.wait()
    pl.semaphore_wait(barrier, 4 + replicas - 1)

    def hand(src, dst, slot, kind, target):
        return pltpu.make_async_remote_copy(
            src_ref=src, dst_ref=dst.at[slot],
            send_sem=send_sem.at[kind, slot], recv_sem=recv_sem.at[kind, slot],
            device_id=(target, r), device_id_type=MESH,
        )

    hand(y1.at[0], y2, 1, 1, before).start()
    hand(c2.at[0], c1, 1, 2, before).start()
    dgain[...] = jnp.zeros_like(dgain)

    def rows_of(tick, replica):
        return pl.ds(pl.multiple_of((tick * replicas + replica) * rows, rows), rows)

    def share(tick, j, kind):
        peer = peers[j]
        peer_core = lax.rem(peer, CORES)
        peer_chip = peer // CORES
        rows_here = rows_of(tick, r)
        if kind == 0:
            src, dst = normed.at[tick, peer_chip], normed_all.at[rows_here]
        elif kind == 1:
            src, dst = second.at[tick, peer_chip], second_all.at[rows_here]
        else:
            cols = pl.ds((kind - 2) * dim, dim)
            src, dst = right.at[tick, peer_core, :, cols], right_all.at[rows_here, cols]
        return pltpu.make_async_remote_copy(
            src_ref=src, dst_ref=dst,
            send_sem=dp_send.at[kind, tick, j], recv_sem=dp_recv.at[kind, tick, j],
            device_id=(s, peer), device_id_type=MESH,
        )

    partner = chip * CORES + CORES - 1 - core
    offsets = [CORES * q for q in range(1, chips)]

    def forward(tick, q):
        source = lax.rem(r + replicas - offsets[q], replicas)
        span = rows_of(tick, source)
        return pltpu.make_async_remote_copy(
            src_ref=normed_all.at[span], dst_ref=normed_all.at[span],
            send_sem=fwd_send.at[tick, q], recv_sem=fwd_recv.at[tick, q],
            device_id=(s, partner), device_id_type=MESH,
        )

    def own_copy(tick, kind):
        if kind == 0:
            src, dst = normed.at[tick, chip], normed_all
        elif kind == 1:
            src, dst = second.at[tick, chip], second_all
        else:
            src, dst = right.at[tick, core], right_all
        return pltpu.make_async_copy(src, dst.at[rows_of(tick, r)], own_sem.at[kind, tick])

    def wanted(j):
        return lax.rem(peers[j], CORES) == CORES - 1

    def near(j):
        return peers[j] == partner

    def norm_start(tick):
        for j in reversed(range(replicas - 1)):
            if j + 1 in offsets:
                share(tick, j, 0).start()
            else:
                @pl.when(near(j))
                def _(j=j):
                    share(tick, j, 0).start()
        own_copy(tick, 0).start()

    def second_start(tick):
        for j in reversed(range(replicas - 1)):
            @pl.when(wanted(j))
            def _(j=j):
                share(tick, j, 1).start()
        own_copy(tick, 1).start()

    def right_start(tick, kind, last_core):
        for j in reversed(range(replicas - 1)):
            @pl.when(wanted(j) if last_core else jnp.logical_not(wanted(j)))
            def _(j=j):
                share(tick, j, kind).start()

    def weights_here(t):
        @pl.when(t == 0)
        def _():
            for copy in w_loads:
                copy.wait()

    def tick_body(t, carry):
        @pl.when(t > 0)
        def _():
            hand(y1.at[0], y1, t, 0, before).wait_recv()

        stream = y1[t].astype(f32)
        scale = lax.rsqrt(jnp.mean(stream * stream, axis=-1, keepdims=True) + epsilon)
        n = (stream * scale * gain_ref[...]).astype(bf16)
        for c in range(chips):
            normed[t, c] = n[:, c * part : (c + 1) * part]
        norm_start(t)

        @pl.when(t > 0)
        def _():
            hand(c2.at[0], c2, t, 3, before).wait_recv()
            hand(y2.at[0], y2, t, 1, before).wait_recv()
            hand(c1.at[0], c1, t, 2, before).wait_recv()

        @pl.when(is_att)
        def _():
            right[t, 1, :, dim:] = c2[t]
            right_start(t, 3, True)
            weights_here(t)
            for j in range(3):
                proj[:, j * dim : (j + 1) * dim] = dot_nn(n, w[j])
            dmix[...] = dot_nt(c2[t], w[3])
            seg = segs[lax.rem(s + t, sections)].astype(f32)
            across = jnp.broadcast_to(seg, (rows, rows))
            row_id = lax.broadcasted_iota(jnp.int32, (rows, rows), 0)
            col_id = lax.broadcasted_iota(jnp.int32, (rows, rows), 1)
            one = ((across == across.T) & (col_id <= row_id)).astype(f32)
            keep = jnp.concatenate([one, one], axis=0)
            lane = lax.broadcasted_iota(jnp.int32, (rows, 2 * head), 1)
            low = lane < head

            def stacked(values):
                return jnp.concatenate(
                    [jnp.where(low, values, 0.0), jnp.where(low, 0.0, values)], axis=0
                )

            def merged(values):
                return jnp.where(low, values[:rows], values[rows:])

            def means(values):
                first = jnp.sum(jnp.where(low, values, 0.0), axis=-1, keepdims=True)
                last = jnp.sum(jnp.where(low, 0.0, values), axis=-1, keepdims=True)
                return first * (1.0 / head), last * (1.0 / head)

            def inv_rms(values):
                first, last = means(values * values)
                return jnp.where(low, lax.rsqrt(first + epsilon), lax.rsqrt(last + epsilon))

            def norm_back(grad, unit, inv):
                first, last = means(grad * unit)
                return inv * (grad - unit * jnp.where(low, first, last))

            def pair(i, carry):
                base = i * 2 * head
                at = [pl.ds(pl.multiple_of(base + j * dim, 2 * head), 2 * head) for j in range(3)]
                q, k = proj[:, at[0]], proj[:, at[1]]
                v = proj[:, at[2]].astype(bf16)
                q_inv, k_inv = inv_rms(q), inv_rms(k)
                q_unit, k_unit = q * q_inv, k * k_inv
                q_two = stacked(q_unit).astype(bf16)
                k_one = k_unit.astype(bf16)
                e = jnp.exp(dot_nt(q_two, k_one) * (1.0 / math.sqrt(head))) * keep
                soft = e * (1.0 / jnp.sum(e, axis=-1, keepdims=True))
                p = soft.astype(bf16)
                o = merged(dot_nn(p, v)).astype(bf16)
                per = part // (2 * head)
                second[t, i // per, :, pl.ds(pl.multiple_of(lax.rem(i, per) * 2 * head, 2 * head), 2 * head)] = o
                do = stacked(dmix[:, at[0]]).astype(bf16)
                dv = dot_tn(p, do)
                dp = dot_nt(do, v).astype(bf16).astype(f32)
                ds = soft * (dp - jnp.sum(dp * soft, axis=-1, keepdims=True))
                ds = (ds * (1.0 / math.sqrt(head))).astype(bf16)
                dq = merged(dot_nn(ds, k_one)).astype(bf16).astype(f32)
                dk = dot_tn(ds, q_two).astype(bf16).astype(f32)
                right[t, 0, :, at[0]] = norm_back(dq, q_unit, q_inv).astype(bf16)
                right[t, 0, :, at[1]] = norm_back(dk, k_unit, k_inv).astype(bf16)
                right[t, 1, :, at[0]] = dv.astype(bf16)
                return carry

            lax.fori_loop(0, HEADS // 2, pair, 0, unroll=4)
            right_start(t, 2, False)
            right_start(t, 3, False)
            right_start(t, 2, True)
            second_start(t)

        @pl.when(jnp.logical_not(is_att))
        def _():
            for c in range(chips):
                second[t, c] = c2[t, :, c * part : (c + 1) * part]
            second_start(t)
            weights_here(t)
            for j in range(2):
                at = pl.ds(j * dim, dim)
                proj[:, at] = dot_nn(n, w[j])
                dmix[...] = dot_nn(c2[t], w[2 + j])

                def strip(i, carry):
                    cols = pl.ds(pl.multiple_of(i * 256, 256), 256)
                    to = pl.ds(pl.multiple_of(j * dim + i * 256, 256), 256)
                    x = proj[:, to]
                    square = x * x
                    tanh = jnp.tanh(GELU_A * x * (1.0 + GELU_B * square))
                    half = 0.5 * (1.0 + tanh)
                    slope = half + 0.5 * x * (1.0 - tanh * tanh) * GELU_A * (1.0 + 3.0 * GELU_B * square)
                    right[t, 1, :, to] = (x * half).astype(bf16)
                    right[t, 0, :, to] = (slope * dmix[:, cols]).astype(bf16)
                    return carry

                lax.fori_loop(0, dim // 256, strip, 0)
                right_start(t, 2 + j, False)
                right_start(t, 2 + j, True)

        own_copy(t, 2).start()

        @pl.when(is_att)
        def _():
            branch = dot_nn(second[t, 0], w[3, :part])
            for c in range(1, chips):
                branch = branch + dot_nn(second[t, c], w[3, c * part : (c + 1) * part])
            y1[t + 1 + TICKS] = (y2[t].astype(f32) - branch).astype(bf16)

        @pl.when(jnp.logical_not(is_att))
        def _():
            branch = dot_nt(right[t, 1, :, :dim], w[2]) + dot_nt(right[t, 1, :, dim:], w[3])
            y1[t + 1 + TICKS] = (y2[t].astype(f32) - branch).astype(bf16)

        made, cot = t + 1 + TICKS, t + 1 + TICKS
        hand(y1.at[made], y1, t + 1, 0, before).start()

        @pl.when(is_att)
        def _():
            dmix[...] = (
                dot_nt(right[t, 0, :, :dim], w[0])
                + dot_nt(right[t, 0, :, dim:], w[1])
                + dot_nt(right[t, 1, :, :dim], w[2])
            )

        @pl.when(jnp.logical_not(is_att))
        def _():
            dmix[...] = dot_nt(right[t, 0, :, :dim], w[0]) + dot_nt(right[t, 0, :, dim:], w[1])

        dn = dmix[...]
        unit = y1[t].astype(f32) * scale
        dgain[...] += jnp.sum(dn * unit, axis=0, keepdims=True)
        weighted = dn * gain_ref[...]
        du = scale * (weighted - unit * jnp.mean(weighted * unit, axis=-1, keepdims=True))
        c2[cot] = (c1[t].astype(f32) + du).astype(bf16)
        hand(c2.at[cot], c2, t + 1, 3, before).start()

        @pl.when(t < TICKS - 1)
        def _():
            hand(y1.at[made], y2, t + 2, 1, before2).start()
            hand(c2.at[cot], c1, t + 2, 2, before2).start()

        for q in range(chips - 1):
            share(t, offsets[q] - 1, 0).wait_recv()
            forward(t, q).start()
        return carry

    lax.fori_loop(0, TICKS, tick_body, 0)

    total = dgain[...].astype(bf16).astype(f32)
    for q in range(replicas):
        dgain_send[q] = jnp.broadcast_to(total[:, q * own : (q + 1) * own], dgain_send.shape[1:])

    def gain_copy(j):
        return pltpu.make_async_remote_copy(
            src_ref=dgain_send.at[peers[j]], dst_ref=dgain_all.at[r],
            send_sem=dg_send.at[j], recv_sem=dg_recv.at[j],
            device_id=(s, peers[j]), device_id_type=MESH,
        )

    for j in range(replicas - 1):
        gain_copy(j).start()
    dgain_all[r] = dgain_send[r]

    def share_wait(tick):
        for kind in (0, 2):
            own_copy(tick, kind).wait()
        for q in range(chips - 1):
            share(tick, offsets[q] - 1, 0).wait_send()
            forward(tick, q).wait()
        for j in reversed(range(replicas - 1)):
            if j + 1 not in offsets:
                @pl.when(near(j))
                def _(j=j):
                    share(tick, j, 0).wait_send()

                @pl.when(lax.rem(r + replicas - j - 1, replicas) == partner)
                def _(j=j):
                    share(tick, j, 0).wait_recv()

    def second_wait(tick):
        own_copy(tick, 1).wait()
        for j in reversed(range(replicas - 1)):
            @pl.when(wanted(j))
            def _(j=j):
                share(tick, j, 1).wait_send()

            @pl.when(core == CORES - 1)
            def _(j=j):
                share(tick, j, 1).wait_recv()

    def piece_wait(tick, piece):
        for j in reversed(range(replicas - 1)):
            share(tick, j, 2 + piece).wait()

        @pl.when(is_att if piece == 1 else jnp.logical_not(is_att))
        def _():
            second_wait(tick)

    tokens = replicas * rows
    chunk = 256

    def accumulate(first, count, fresh, low, high):
        span = pl.ds(first * tokens, count * tokens)

        def strip(i, carry):
            cols = pl.ds(pl.multiple_of(i * chunk, chunk), chunk)
            use_normed = jnp.logical_or(core == 0, jnp.logical_and(is_att, i < dim // chunk))

            @pl.when(use_normed)
            def _():
                value = dot_tn(normed_all[span], right_all[span, cols])
                acc[:, cols] = value if fresh else acc[:, cols] + value

            @pl.when(jnp.logical_not(use_normed))
            def _():
                value = dot_tn(second_all[span], right_all[span, cols])
                acc[:, cols] = value if fresh else acc[:, cols] + value

            return carry

        lax.fori_loop(low // chunk, high // chunk, strip, 0)

    for tick in range(TICKS - 1):
        share_wait(tick)
        for piece in range(2):
            piece_wait(tick, piece)
    accumulate(0, TICKS - 1, True, 0, wide)

    for j in range(replicas - 1):
        gain_copy(j).wait()
    gain_sum = dgain_all[0, :1]
    for q in range(1, replicas):
        gain_sum = gain_sum + dgain_all[q, :1]
    grad_scale = 1.0 / math.sqrt(TICKS * rows * replicas)
    gain_grads[...] = gain_sum * grad_scale

    mine = pl.ds(pl.multiple_of(core * own, own), own)
    other = CORES - 1 - core
    theirs = pl.ds(pl.multiple_of(other * own, own), own)

    def final(piece):
        cols = pl.ds(pl.multiple_of(core * wide + piece * dim, dim), dim)
        return pltpu.make_async_remote_copy(
            src_ref=done.at[:, pl.ds(piece * dim, dim)], dst_ref=grads.at[:, cols],
            send_sem=fin_send.at[piece], recv_sem=fin_recv.at[piece],
            device_id=(s, partner), device_id_type=MESH,
        )

    share_wait(TICKS - 1)
    for piece in range(2):
        piece_wait(TICKS - 1, piece)
        accumulate(TICKS - 1, 1, False, piece * dim, (piece + 1) * dim)
        here = pl.ds(piece * dim, dim)
        done[:, here] = (acc[theirs, here] * grad_scale).astype(bf16)
        final(piece).start()
        cols = pl.ds(pl.multiple_of(core * wide + piece * dim, dim), dim)
        grads[:, cols] = (acc[mine, here] * grad_scale).astype(bf16)

    hand(y1.at[0], y1, TICKS, 0, before).wait_recv()
    hand(c2.at[0], c2, TICKS, 3, before).wait_recv()
    hand(y2.at[0], y2, TICKS, 1, before).wait_recv()
    hand(c1.at[0], c1, TICKS, 2, before).wait_recv()
    out_streams[0] = y1[TICKS]
    out_streams[1] = y2[TICKS]
    out_cotangents[0] = c1[TICKS]
    out_cotangents[1] = c2[TICKS]
    for slot in range(1, TICKS + 1):
        hand(y1.at[0], y1, slot, 0, before).wait_send()
        hand(c2.at[0], c2, slot, 3, before).wait_send()
        hand(y1.at[0], y2, slot, 1, before).wait_send()
        hand(c2.at[0], c1, slot, 2, before).wait_send()
    for piece in range(2):
        final(piece).wait()


def shards(streams, cotangents, weights, norm_gains, segment_ids):
    sections = lax.axis_size("section")
    replicas = lax.axis_size("dp")
    chips = replicas // CORES
    rows, dim = streams.shape[3:]
    full = weights.shape[2]
    wide = full // CORES
    part = dim // chips
    own = dim // replicas
    tokens = TICKS * replicas * rows
    dma = pltpu.SemaphoreType.DMA
    vmem = pl.BlockSpec(memory_space=pltpu.VMEM)
    hbm = pl.BlockSpec(memory_space=pl.ANY)
    flops = 2 * TICKS * rows * dim * full * 3
    out_streams, out_cotangents, grads, gains = pl.pallas_call(
        partial(kernel, sections, replicas),
        out_shape=(
            jax.ShapeDtypeStruct((2, rows, dim), bf16),
            jax.ShapeDtypeStruct((2, rows, dim), bf16),
            jax.ShapeDtypeStruct((own, full), bf16),
            jax.ShapeDtypeStruct((1, own), f32),
        ),
        in_specs=[hbm, hbm, hbm, vmem, vmem],
        out_specs=(vmem, vmem, vmem, vmem),
        scratch_shapes=[
            pltpu.VMEM((4, dim, dim), bf16),
            pltpu.VMEM((2 * TICKS + 1, rows, dim), bf16),
            pltpu.VMEM((TICKS + 1, rows, dim), bf16),
            pltpu.VMEM((TICKS + 1, rows, dim), bf16),
            pltpu.VMEM((2 * TICKS + 1, rows, dim), bf16),
            pltpu.VMEM((rows, 3 * dim), f32),
            pltpu.VMEM((rows, dim), f32),
            pltpu.VMEM((TICKS, CORES, rows, wide), bf16),
            pltpu.VMEM((TICKS, chips, rows, part), bf16),
            pltpu.VMEM((TICKS, chips, rows, part), bf16),
            pltpu.VMEM((tokens, wide), bf16),
            pltpu.VMEM((tokens, part), bf16),
            pltpu.VMEM((tokens, part), bf16),
            pltpu.VMEM((1, dim), f32),
            pltpu.VMEM((replicas, 8, own), f32),
            pltpu.VMEM((replicas, 8, own), f32),
            pltpu.VMEM((part, wide), f32),
            pltpu.VMEM((own, wide), bf16),
            dma((4,)),
            dma((4,)),
            dma((4, TICKS + 1)),
            dma((4, TICKS + 1)),
            dma((3, TICKS)),
            dma((4, TICKS, replicas - 1)),
            dma((4, TICKS, replicas - 1)),
            dma((TICKS, chips - 1)),
            dma((TICKS, chips - 1)),
            dma((replicas - 1,)),
            dma((replicas - 1,)),
            dma((2,)),
            dma((2,)),
        ],
        compiler_params=pltpu.CompilerParams(
            collective_id=0, has_side_effects=True, vmem_limit_bytes=56 * 1024 * 1024
        ),
        cost_estimate=pl.CostEstimate(
            flops=flops, bytes_accessed=2 * dim * full, transcendentals=0
        ),
        name="ticks",
    )(
        streams[:, 0, 0],
        cotangents[:, 0, 0],
        weights[0],
        norm_gains,
        segment_ids,
    )
    return (
        out_streams[:, None, None],
        out_cotangents[:, None, None],
        grads[None],
        gains,
    )


def solution(mesh):
    placed = (
        P(None, "section", "dp", None, None),
        P(None, "section", "dp", None, None),
        P("section", None, None),
        P("section", None),
        P(None, "dp", None),
    )
    return jax.shard_map(
        shards,
        mesh=mesh,
        in_specs=placed,
        out_specs=(
            P(None, "section", "dp", None, None),
            P(None, "section", "dp", None, None),
            P("section", "dp", None),
            P("section", "dp"),
        ),
        check_vma=False,
    )
```
